32 devices in a mesh: row: 16 (over z, y, core), col: 2 (over x).
Axes of the slice: x: 2, y: 2, z: 4, core: 2. Of those that a mesh axis runs over, the one named last changes fastest.
Arguments:
- integrals: bfloat16 [32768, 32768], P('row', 'col'), may hold values from -0.03125 to 0.03125
- amplitudes: bfloat16 [32768, 1024], P(('col', 'row')), may hold values from -6 to 6
- source: float32 [32768, 1024], P(('row', 'col')), may hold values from -6 to 6
- occ_energy: float32 [64], replicated, may hold values from -2.5 to -0.5
- vir_energy: float32 [512], replicated, may hold values from 0.3 to 3
- col_energy: float32 [1024], replicated, may hold values from 0.8 to 3
Outputs:
- new_amplitudes: float32 [32768, 1024], P(('row', 'col'))
The draws below stay inside these ranges and needn't reach their ends.
All inputs are finite; a program needn't handle non-finite values.
Results may differ from the reference program's by a relative error of at most 0.0003.
Values may be sent and summed in bfloat16 or wider, within the bound.
A program may use at most 320 MiB of HBM per device.

```python
import math
import jax
import jax.numpy as jnp
from jax import lax

OCC = 64
VIRT = 512
COLS = 1024
PAIRS = 32768


def levels(stream_key, extent, split, low, largest):
    factor_of, own = 1.0, jax.random.fold_in(stream_key, 6)
    for axis_at, shards_of in split:
        steps = jnp.exp(jax.random.uniform(jax.random.fold_in(own, axis_at), (shards_of,), jnp.float32, low / len(split), largest / len(split)))
        factor_of = factor_of * jnp.repeat(steps, extent[axis_at] // shards_of).reshape([-1 if axis == axis_at else 1 for axis in range(len(extent))])
    return factor_of


def bell_draw(stream_key, shape, deviation, most, pieces=(), held_as=jnp.bfloat16):
    values = jax.random.normal(stream_key, shape, jnp.float32) * deviation
    if len(pieces) > 0:
        values = levels(stream_key, shape, pieces, -0.22, 0.18) * values
    return jnp.clip(values, min=-most, max=most).astype(held_as)


def setup_inputs(seed: int = 0) -> dict:
    splits = jax.random.split(jax.random.key(seed), 7)
    integrals = bell_draw(splits[0], (PAIRS, PAIRS), PAIRS ** -0.5, 0.03125, ((0, 16), (1, 2)))
    amplitudes = bell_draw(splits[1], (PAIRS, COLS), 1.0, 6.0, ((0, 32),))
    source = bell_draw(splits[2], (PAIRS, COLS), 1.0, 6.0, ((0, 32),), jnp.float32)
    occ_energy = jnp.clip(jax.random.uniform(splits[3], (OCC,), jnp.float32, -2.5, -0.5), -2.5, -0.5)
    vir_energy = jnp.clip(jnp.exp(jax.random.uniform(splits[4], (VIRT,), jnp.float32, math.log(0.3), math.log(3.0))), 0.3, 3.0)
    col_energy = jnp.clip(jax.random.uniform(splits[5], (COLS,), jnp.float32, 0.8, 3.0), 0.8, 3.0)
    return {"integrals": integrals, "amplitudes": amplitudes, "source": source, "occ_energy": occ_energy, "vir_energy": vir_energy, "col_energy": col_energy}


def reference(integrals, amplitudes, source, occ_energy, vir_energy, col_energy):
    cycle_term = jnp.dot(integrals, amplitudes, preferred_element_type=jnp.float32)
    blocks = integrals.reshape(OCC, VIRT, OCC, VIRT)
    amp_blocks = amplitudes.astype(jnp.float32).reshape(OCC, VIRT, COLS)

    def one_occupied(block):
        return jnp.einsum("bja,jbc->ac", block.astype(jnp.float32), amp_blocks, precision=lax.Precision.HIGHEST)

    exchange_term = lax.map(one_occupied, blocks).reshape(PAIRS, COLS)
    denom = vir_energy[None, :, None] - occ_energy[:, None, None] + col_energy[None, None, :]
    denom = denom.reshape(PAIRS, COLS)
    return -(source + cycle_term + exchange_term) / denom
```

```python
import functools

import jax
import jax.numpy as jnp
from jax import lax
from jax.experimental import pallas as pl
from jax.experimental.pallas import tpu as pltpu
from jax.sharding import PartitionSpec as P

VMEM_BYTES = 58 * 1024 * 1024
SMALL = jnp.float8_e5m2
REST_SCALE = 2.0**28
AMP_SCALE = 2.0**12
UNSCALE = 1.0 / (REST_SCALE * AMP_SCALE)


def pair_sum_kernel(block_ref, head_ref, rest_ref, *, virt):
    for at in range(block_ref.shape[1] // virt):
        columns = slice(at * virt, (at + 1) * virt)
        block = block_ref[:, columns]
        both = block.astype(jnp.float32) + block.T.astype(jnp.float32)
        head = both.astype(jnp.bfloat16)
        rest = (both - head.astype(jnp.float32)) * REST_SCALE
        head_ref[:, columns] = head
        rest_ref[:, columns] = rest.astype(SMALL)


def pair_sum(integrals, virt):
    rows, columns = integrals.shape
    wide = min(columns, 4 * virt)
    out_map = lambda i, j: (i, j)
    kernel = functools.partial(pair_sum_kernel, virt=virt)
    return pl.pallas_call(
        kernel,
        grid=(rows // virt, columns // wide),
        in_specs=[pl.BlockSpec((virt, wide), out_map)],
        out_specs=[pl.BlockSpec((virt, wide), out_map)] * 2,
        out_shape=[
            jax.ShapeDtypeStruct((rows, columns), jnp.bfloat16),
            jax.ShapeDtypeStruct((rows, columns), SMALL),
        ],
        compiler_params=pltpu.CompilerParams(vmem_limit_bytes=VMEM_BYTES),
        cost_estimate=pl.CostEstimate(
            flops=rows * columns * 8,
            bytes_accessed=rows * columns * 5,
            transcendentals=0,
        ),
        name="pair_sum",
    )(integrals)


def product_kernel(where_ref, head_ref, rest_ref, amp_ref, *others):
    out_ref = others[-1]
    amp = amp_ref[...]
    small = (amp.astype(jnp.float32) * AMP_SCALE).astype(SMALL)
    fine = jnp.dot(rest_ref[...], small, preferred_element_type=jnp.float32)
    term = jnp.dot(head_ref[...], amp, preferred_element_type=jnp.float32) + fine * UNSCALE

    @pl.when(pl.program_id(0) == 0)
    def _():
        out_ref[...] = term if len(others) == 1 else others[0][...] + term

    @pl.when(pl.program_id(0) != 0)
    def _():
        out_ref[...] += term


def product(where, head, rest, amp, so_far, rows, depth, parts, part):
    columns = amp.shape[1]
    steps = amp.shape[0] // depth
    left = pl.BlockSpec((rows, depth), lambda k, w: (w[0], k * parts + part))
    in_specs = [left, left, pl.BlockSpec((depth, columns), lambda k, w: (k, 0))]
    args = [head, rest, amp]
    if so_far is not None:
        in_specs.append(pl.BlockSpec((rows, columns), lambda k, w: (w[0], 0)))
        args.append(so_far)
    return pl.pallas_call(
        product_kernel,
        grid_spec=pltpu.PrefetchScalarGridSpec(
            num_scalar_prefetch=1,
            grid=(steps,),
            in_specs=in_specs,
            out_specs=pl.BlockSpec((rows, columns), lambda k, w: (0, 0)),
        ),
        out_shape=jax.ShapeDtypeStruct((rows, columns), jnp.float32),
        compiler_params=pltpu.CompilerParams(vmem_limit_bytes=VMEM_BYTES),
        cost_estimate=pl.CostEstimate(
            flops=3 * rows * columns * amp.shape[0],
            bytes_accessed=rows * amp.shape[0] * 3,
            transcendentals=0,
        ),
        name="product",
    )(where, head, rest, amp, *([] if so_far is None else [so_far]))


def per_device(integrals, amplitudes, source, occ_energy, vir_energy, col_energy):
    virt = vir_energy.shape[0]
    cols = lax.axis_size("col")
    me = lax.axis_index("col")
    rows, depth = integrals.shape
    out_rows, columns = source.shape
    amp_rows = amplitudes.shape[0]
    half = columns // 2
    parts = 2 if amp_rows % (2 * 256) == 0 else 1
    sub = amp_rows // parts

    gather = lambda x: lax.all_gather(x, "row", axis=0, tiled=True)
    amp_first = gather(amplitudes[:, :half])
    amp_later = [gather(amplitudes[p * sub : (p + 1) * sub, half:]) for p in range(parts)]

    head, rest = pair_sum(integrals, virt)

    deep = min(depth, 1024)
    whole = jnp.zeros((1,), jnp.int32)
    first = product(whole, head, rest, amp_first, None, rows, deep, 1, 0)

    def swap(block, step):
        order = [(i, (i + step) % cols) for i in range(cols)]
        return lax.ppermute(block, "col", order)

    def share(total, step):
        return lax.dynamic_slice_in_dim(total, lax.rem(me + step, cols) * out_rows, out_rows, 0)

    got_first = [swap(share(first, s).astype(jnp.float16), s) for s in range(1, cols)]
    kept_first = share(first, 0)

    later = None
    for p in range(parts - 1):
        later = product(whole, head, rest, amp_later[p], later, rows, sub, parts, p)
    last_depth = sub if parts > 1 else deep
    got_later = []
    for s in list(range(1, cols)) + [0]:
        where = lax.rem(me + s, cols).reshape(1)
        block = product(where, head, rest, amp_later[-1], later, out_rows, last_depth, parts, parts - 1)
        if s > 0:
            got_later.append(swap(block.astype(jnp.float16), s))
        else:
            kept_later = block

    def total(kept, got):
        for g in got:
            kept = kept + g.astype(jnp.float32)
        return kept

    summed = jnp.concatenate([total(kept_first, got_first), total(kept_later, got_later)], axis=1)
    start = (lax.axis_index("row") * cols + me) * out_rows
    vir_all = jnp.tile(vir_energy, occ_energy.shape[0])
    occ_all = jnp.repeat(occ_energy, virt)
    vir_part = lax.dynamic_slice_in_dim(vir_all, start, out_rows, 0)
    occ_part = lax.dynamic_slice_in_dim(occ_all, start, out_rows, 0)
    denom = vir_part[:, None] - occ_part[:, None] + col_energy[None, :]
    return -(source + summed) / denom


def solution(mesh):
    in_specs = (P("row", "col"), P(("col", "row"), None), P(("row", "col"), None), P(), P(), P())
    out_specs = P(("row", "col"), None)
    return jax.shard_map(
        per_device, mesh=mesh, in_specs=in_specs, out_specs=out_specs, check_vma=False
    )
```
